32 devices in a mesh: blk: 16 (over z, y, x), dp: 2 (over core).
Axes of the slice: x: 2, y: 2, z: 4, core: 2. Of those that a mesh axis runs over, the one named last changes fastest.
Arguments:
- tokens: bfloat16 [7168, 2048], P('blk', 'dp'), may hold values from -6 to 6
- cotangent: bfloat16 [7168, 2048], P('blk', 'dp'), may hold values from -6 to 6
- block_tokens: int32 [224, 64], P('blk'), may hold values from 0 to 447, as said below
- block_expert: int32 [224], P('blk'), may hold values from -1 to 15, as said below
- block_gate: bfloat16 [224, 64], P('blk'), may hold values from 0.099609375 to 1
- w_gate: bfloat16 [16, 2048, 768], P('blk', None, 'dp'), may hold values from -0.125 to 0.125
- w_up: bfloat16 [16, 2048, 768], P('blk', None, 'dp'), may hold values from -0.125 to 0.125
- w_down: bfloat16 [16, 768, 2048], P('blk', 'dp'), may hold values from -0.21875 to 0.21875
Outputs:
- mixed: bfloat16 [7168, 2048], P('blk', 'dp')
- grad_tokens: bfloat16 [7168, 2048], P('blk', 'dp')
- grad_gate: bfloat16 [16, 2048, 768], P('blk', None, 'dp')
- grad_up: bfloat16 [16, 2048, 768], P('blk', None, 'dp')
- grad_down: bfloat16 [16, 768, 2048], P('blk', 'dp')
The draws below stay inside these ranges and needn't reach their ends.
Inputs may be any that keep to these rules, and one draw needn't show every extreme that they name: `block_expert`: the slots of device b (slots b * 14 to (b + 1) * 14 - 1) hold first between 1 and 7 blocks of expert b, then between 1 and 7 blocks of expert (b + 1) mod 16, then empty slots marked -1; device 0 holds 7 blocks of each of its two experts. `block_tokens`: indices into the 448 tokens of the slot's own device; the live blocks of one expert on one device name distinct tokens.
All inputs are finite; a program needn't handle non-finite values.
Results may differ from the reference program's by a relative error of at most 0.0066.
Values may be sent and summed in bfloat16 or wider, within the bound.
No kernel may reach another device: no remote copies, remote signals or barrier semaphores. Data moves between devices by JAX's collectives and lax.ppermute only.
A program may use at most 128 MiB of HBM per device.

```python
import math
from functools import partial
import jax
import jax.numpy as jnp
from jax import lax

D = 2048
F = 768
BLOCK = 64
TOK_DEV = 448
EXPERTS = 16
TOKENS = 7168
SPAN = 7
SLOTS = 14
ALL_SLOTS = 224


def block_counts(key):
    base_key = jax.random.fold_in(key, 7)
    key_list = jax.random.split(base_key, 4)
    device_ids = jnp.arange(EXPERTS, dtype=jnp.int32)

    def draw_count(first_key, second_key):
        left_term = jax.random.randint(first_key, (EXPERTS,), 0, SPAN)
        right_term = jax.random.randint(second_key, (EXPERTS,), 0, SPAN)
        counts = 1 + left_term * right_term // (SPAN - 1)
        return jnp.where(device_ids == 0, SPAN, counts).astype(jnp.int32)
    return (draw_count(key_list[0], key_list[1]), draw_count(key_list[2], key_list[3]))


def draw_block_expert(key, part):
    own_counts, next_counts = block_counts(key)
    slot_ids = jnp.arange(SLOTS, dtype=jnp.int32)[None, :]
    owners = jnp.arange(EXPERTS, dtype=jnp.int32)[:, None]
    own_end = own_counts[:, None]
    next_end = own_end + next_counts[:, None]
    labels = jnp.where(slot_ids < own_end, owners, jnp.where(slot_ids < next_end, (owners + 1) % EXPERTS, -1))
    return labels.reshape(EXPERTS * SLOTS).astype(jnp.int32)


def draw_block_tokens(key, part):
    own_counts, next_counts = block_counts(key)
    perm_keys = jax.random.split(jax.random.fold_in(key, 11), 2 * EXPERTS)
    orders = jax.vmap(partial(jax.random.permutation, x=TOK_DEV))(perm_keys)
    blocks = orders.reshape(EXPERTS, 2 * SPAN, BLOCK)
    slot_ids = jnp.arange(SLOTS, dtype=jnp.int32)[None, :]
    own_end = own_counts[:, None]
    next_end = own_end + next_counts[:, None]
    source = jnp.where(slot_ids < own_end, slot_ids, jnp.where(slot_ids < next_end, SPAN + slot_ids - own_end, slot_ids))
    picked = jnp.take_along_axis(blocks, source[:, :, None], axis=1)
    return picked.reshape(EXPERTS * SLOTS, BLOCK).astype(jnp.int32)


def block_scale(key, shape, cuts, least, high):
    factor_of = 1.0
    for position, parts in cuts:
        heights = jax.random.uniform(jax.random.fold_in(jax.random.fold_in(key, 6), position), (parts,), jnp.float32, least / len(cuts), high / len(cuts))
        factor_of = factor_of * jnp.repeat(jnp.exp(heights), shape[position] // parts).reshape((-1,) + (1,) * (len(shape) - 1 - position))
    return factor_of


def noise(own_key, dims, spread, reach, pieces=(), kind=jnp.bfloat16):
    array = jax.random.normal(own_key, dims, jnp.float32) * spread
    if len(pieces) > 0:
        array = block_scale(own_key, dims, pieces, -0.22, 0.18) * array
    return jnp.clip(array, min=-reach, max=reach).astype(kind)


def setup_inputs(seed: int = 0) -> dict:
    splits = jax.random.split(jax.random.key(seed), 9)
    return {
        "tokens": noise(splits[0], (TOKENS, D), 1.0, 6.0, ((0, 16), (1, 2))),
        "cotangent": noise(splits[1], (TOKENS, D), 1.0, 6.0, ((0, 16), (1, 2))),
        "block_tokens": draw_block_tokens(jax.random.fold_in(splits[8], 71), 0),
        "block_expert": draw_block_expert(jax.random.fold_in(splits[8], 71), 0),
        "block_gate": jnp.clip(jnp.exp(math.log(1.0) - 2.306499 * jax.random.uniform(splits[4], (ALL_SLOTS, BLOCK), jnp.float32) ** block_scale(splits[4], (ALL_SLOTS, BLOCK), ((0, 16),), -0.2, 0.2)), 0.099609375, 1.0).astype(jnp.bfloat16),
        "w_gate": noise(splits[5], (EXPERTS, D, F), D ** -0.5, 0.125, ((0, 16), (2, 2))),
        "w_up": noise(splits[6], (EXPERTS, D, F), D ** -0.5, 0.125, ((0, 16), (2, 2))),
        "w_down": noise(splits[7], (EXPERTS, F, D), F ** -0.5, 0.21875, ((0, 16), (1, 2))),
    }


def silu_parts(pre_value):
    sigmoid_value = 1.0 / (1.0 + jnp.exp(-pre_value))
    active = pre_value * sigmoid_value
    slope_term = sigmoid_value * (1.0 + pre_value * (1.0 - sigmoid_value))
    return active, slope_term


def contract_rows(left_side, right_side):
    return lax.dot_general(left_side, right_side, (((1,), (1,)), ((), ())), preferred_element_type=jnp.float32)


def contract_cols(left_side, right_side):
    return lax.dot_general(left_side, right_side, (((0,), (0,)), ((), ())), preferred_element_type=jnp.float32)


def block_pass(rows_in, rows_cot, weight_row, w_first, w_second, w_third):
    gate_pre = jnp.dot(rows_in, w_first, preferred_element_type=jnp.float32)
    up_pre = jnp.dot(rows_in, w_second, preferred_element_type=jnp.float32)
    active, slope_term = silu_parts(gate_pre)
    hidden = (active * up_pre).astype(jnp.bfloat16)
    column = weight_row[:, None]
    out_rows = column * jnp.dot(hidden, w_third, preferred_element_type=jnp.float32)
    scaled = (column * rows_cot.astype(jnp.float32)).astype(jnp.bfloat16)
    back_hidden = contract_rows(scaled, w_third)
    grad_gate_pre = (back_hidden * up_pre * slope_term).astype(jnp.bfloat16)
    grad_up_pre = (back_hidden * active).astype(jnp.bfloat16)
    back_rows = contract_rows(grad_gate_pre, w_first) + contract_rows(grad_up_pre, w_second)
    return out_rows, back_rows, contract_cols(rows_in, grad_gate_pre), contract_cols(rows_in, grad_up_pre), contract_cols(hidden, scaled)


def group_pass(features, cotangents, slot_tokens, slot_gate, slot_expert, first_slot, wanted, w_first, w_second, w_third):
    span_blocks = slot_tokens.shape[0] // 2
    row_index = lax.dynamic_slice_in_dim(slot_tokens, first_slot, span_blocks, 0).reshape(-1)
    live_mask = (lax.dynamic_slice_in_dim(slot_expert, first_slot, span_blocks, 0) == wanted).astype(jnp.float32)
    gate_rows = lax.dynamic_slice_in_dim(slot_gate, first_slot, span_blocks, 0).astype(jnp.float32)
    weight_row = (gate_rows * live_mask[:, None]).reshape(-1)
    rows_in = jnp.take(features, row_index, axis=0)
    rows_cot = jnp.take(cotangents, row_index, axis=0)
    out_rows, back_rows, grad_first, grad_second, grad_third = block_pass(rows_in, rows_cot, weight_row, w_first, w_second, w_third)
    zero_rows = jnp.zeros((features.shape[0], out_rows.shape[1]), jnp.float32)
    return zero_rows.at[row_index].add(out_rows), zero_rows.at[row_index].add(back_rows), grad_first, grad_second, grad_third


def rounded(values):
    return lax.optimization_barrier(values.astype(jnp.bfloat16)).astype(jnp.float32)


def reference(tokens, cotangent, block_tokens, block_expert, block_gate, w_gate, w_up, w_down):
    token_rows = tokens.reshape(EXPERTS, TOK_DEV, D)
    cot_rows = cotangent.reshape(EXPERTS, TOK_DEV, D)
    slot_tokens = block_tokens.reshape(EXPERTS, SLOTS, BLOCK)
    slot_expert = block_expert.reshape(EXPERTS, SLOTS)
    slot_gate = block_gate.reshape(EXPERTS, SLOTS, BLOCK)

    def per_expert(expert_id):
        prior_expert = (expert_id + EXPERTS - 1) % EXPERTS
        own_total = group_pass(token_rows[expert_id], cot_rows[expert_id], slot_tokens[expert_id], slot_gate[expert_id], slot_expert[expert_id], jnp.int32(0), expert_id, w_gate[expert_id], w_up[expert_id], w_down[expert_id])
        prior_first = jnp.sum((slot_expert[prior_expert] == prior_expert).astype(jnp.int32))
        lent_total = group_pass(token_rows[prior_expert], cot_rows[prior_expert], slot_tokens[prior_expert], slot_gate[prior_expert], slot_expert[prior_expert], prior_first, expert_id, w_gate[expert_id], w_up[expert_id], w_down[expert_id])
        grad_first = (rounded(own_total[2]) + rounded(lent_total[2])).astype(jnp.bfloat16)
        grad_second = (rounded(own_total[3]) + rounded(lent_total[3])).astype(jnp.bfloat16)
        grad_third = (rounded(own_total[4]) + rounded(lent_total[4])).astype(jnp.bfloat16)
        return own_total[0], own_total[1], lent_total[0], lent_total[1], grad_first, grad_second, grad_third

    results = lax.map(per_expert, jnp.arange(EXPERTS, dtype=jnp.int32))
    own_out, own_back, lent_out, lent_back, grad_gate, grad_up, grad_down = results
    mixed = (own_out + jnp.roll(lent_out, -1, axis=0)).reshape(TOKENS, D).astype(jnp.bfloat16)
    grad_tokens = (own_back + jnp.roll(lent_back, -1, axis=0)).reshape(TOKENS, D).astype(jnp.bfloat16)
    return (mixed, grad_tokens, grad_gate, grad_up, grad_down)
```

```python
import jax
import jax.numpy as jnp
from jax import lax
from jax.sharding import PartitionSpec as P


def passed_along(block, axis, distance):
    size = lax.axis_size(axis)
    return lax.ppermute(block, axis, [((i - distance) % size, i) for i in range(size)])


def partner(block):
    return passed_along(block, "dp", 1)


def contract_rows(left_side, right_side):
    return lax.dot_general(
        left_side, right_side, (((1,), (1,)), ((), ())), preferred_element_type=jnp.float32
    )


def contract_cols(left_side, right_side):
    return lax.dot_general(
        left_side, right_side, (((0,), (0,)), ((), ())), preferred_element_type=jnp.float32
    )


def matmul(left_side, right_side):
    return jnp.dot(left_side, right_side, preferred_element_type=jnp.float32)


def forward(rows_in, w_first, w_second):
    gate_pre = matmul(rows_in, w_first)
    up_pre = matmul(rows_in, w_second)
    sigmoid_value = 1.0 / (1.0 + jnp.exp(-gate_pre))
    active = gate_pre * sigmoid_value
    slope_term = sigmoid_value * (1.0 + gate_pre * (1.0 - sigmoid_value))
    return active, slope_term, up_pre, (active * up_pre).astype(jnp.bfloat16)


def backward(scaled, w_third, active, slope_term, up_pre):
    back_hidden = contract_rows(scaled, w_third)
    grad_gate_pre = (back_hidden * up_pre * slope_term).astype(jnp.bfloat16)
    grad_up_pre = (back_hidden * active).astype(jnp.bfloat16)
    return grad_gate_pre, grad_up_pre


def rounded(values):
    return lax.optimization_barrier(values.astype(jnp.bfloat16)).astype(jnp.float32)


def on_device(tokens, cotangent, block_tokens, block_expert, block_gate, w_gate, w_up, w_down):
    size = lax.axis_size("blk")
    me = lax.axis_index("blk")
    half = lax.axis_index("dp")
    count, width = tokens.shape
    w_first, w_second, w_third = w_gate[0], w_up[0], w_down[0]

    def whole(mine, other):
        return jnp.where(
            half == 0,
            jnp.concatenate([mine, other], axis=1),
            jnp.concatenate([other, mine], axis=1),
        )

    def columns(weight, side):
        return lax.dynamic_slice_in_dim(weight, side * width, width, 1)

    def rows(weight, side):
        return lax.dynamic_slice_in_dim(weight, side * width, width, 0)

    def summed(part):
        return part(half) + partner(part(1 - half).astype(jnp.bfloat16)).astype(jnp.float32)

    gates = block_gate.astype(jnp.float32)
    hit = block_tokens.reshape(1, -1) == jnp.arange(count, dtype=jnp.int32)[:, None]

    def token_gate(expert):
        live = jnp.where((block_expert == expert)[:, None], gates, 0.0).reshape(1, -1)
        return jnp.sum(jnp.where(hit, live, 0.0), axis=1, keepdims=True)

    gate_own = token_gate(me)
    gate_next = token_gate(lax.rem(me + 1, size))

    guest_tokens = passed_along(tokens, "blk", 1)
    cot = cotangent.astype(jnp.float32)
    guest_scaled = passed_along((gate_next * cot).astype(jnp.bfloat16), "blk", 1)

    features = whole(tokens, partner(tokens))
    cotangents = whole(cotangent, partner(cotangent))
    scaled = (gate_own * cotangents.astype(jnp.float32)).astype(jnp.bfloat16)
    active, slope_term, up_pre, hidden = forward(features, w_first, w_second)
    own_out = gate_own * summed(lambda side: matmul(hidden, columns(w_third, side)))
    grad_one, grad_two = backward(scaled, w_third, active, slope_term, up_pre)
    own_back = summed(
        lambda side: contract_rows(grad_one, rows(w_first, side))
        + contract_rows(grad_two, rows(w_second, side))
    )
    own_grads = (
        contract_cols(features, grad_one),
        contract_cols(features, grad_two),
        contract_cols(hidden, scaled),
    )

    guest_features = whole(guest_tokens, partner(guest_tokens))
    active, slope_term, up_pre, guest_hidden = forward(guest_features, w_first, w_second)
    guest_out = summed(lambda side: matmul(guest_hidden, columns(w_third, side)))
    came_out = passed_along(guest_out.astype(jnp.bfloat16), "blk", -1)

    guest_cot = whole(guest_scaled, partner(guest_scaled))
    guest_one, guest_two = backward(guest_cot, w_third, active, slope_term, up_pre)
    guest_back = summed(
        lambda side: contract_rows(guest_one, rows(w_first, side))
        + contract_rows(guest_two, rows(w_second, side))
    )
    came_back = passed_along(guest_back.astype(jnp.bfloat16), "blk", -1)
    guest_grads = (
        contract_cols(guest_features, guest_one),
        contract_cols(guest_features, guest_two),
        contract_cols(guest_hidden, guest_cot),
    )

    outputs = own_out + gate_next * came_out.astype(jnp.float32)
    backs = own_back + came_back.astype(jnp.float32)
    grads = tuple(
        (rounded(own) + rounded(guest)).astype(jnp.bfloat16)[None]
        for own, guest in zip(own_grads, guest_grads)
    )
    return (outputs.astype(jnp.bfloat16), backs.astype(jnp.bfloat16)) + grads


def solution(mesh):
    in_specs = (
        P("blk", "dp"),
        P("blk", "dp"),
        P("blk", None),
        P("blk"),
        P("blk", None),
        P("blk", None, "dp"),
        P("blk", None, "dp"),
        P("blk", "dp", None),
    )
    out_specs = (
        P("blk", "dp"),
        P("blk", "dp"),
        P("blk", None, "dp"),
        P("blk", None, "dp"),
        P("blk", "dp", None),
    )
    return jax.shard_map(
        on_device, mesh=mesh, in_specs=in_specs, out_specs=out_specs, check_vma=False
    )
```

```python
import jax
import jax.numpy as jnp
from jax import lax
from jax.experimental import pallas as pl
from jax.experimental.pallas import tpu as pltpu
from jax.sharding import PartitionSpec as P

BF16 = jnp.bfloat16
F32 = jnp.float32
VMEM = pl.BlockSpec(memory_space=pltpu.VMEM)
SMEM = pl.BlockSpec(memory_space=pltpu.SMEM)
ANY = pl.BlockSpec(memory_space=pl.ANY)


def passed_along(block, axis, distance):
    size = lax.axis_size(axis)
    return lax.ppermute(block, axis, [((i - distance) % size, i) for i in range(size)])


def partner(block, pieces=1):
    if pieces == 1:
        return passed_along(block, "dp", 1)
    step = block.shape[0] // pieces
    swapped = [
        passed_along(block[i * step : (i + 1) * step], "dp", 1) for i in range(pieces)
    ]
    return jnp.concatenate(swapped, axis=0)


def matmul(left_side, right_side):
    return jnp.dot(left_side, right_side, preferred_element_type=F32)


def contract_rows(left_side, right_side):
    return lax.dot_general(
        left_side, right_side, (((1,), (1,)), ((), ())), preferred_element_type=F32
    )


def contract_cols(left_side, right_side):
    return lax.dot_general(
        left_side, right_side, (((0,), (0,)), ((), ())), preferred_element_type=F32
    )


def call(body, outs, specs, *operands, name, limit=48, flops=1):
    return pl.pallas_call(
        body,
        out_shape=[jax.ShapeDtypeStruct(shape, kind) for shape, kind in outs],
        in_specs=specs,
        out_specs=[VMEM] * len(outs),
        compiler_params=pltpu.CompilerParams(vmem_limit_bytes=limit * 2**20),
        cost_estimate=pl.CostEstimate(flops=flops, bytes_accessed=1, transcendentals=0),
        name=name,
    )(*operands)


def after(block, ready):
    return pl.pallas_call(
        lambda *refs: None,
        out_shape=jax.ShapeDtypeStruct(block.shape, block.dtype),
        in_specs=[ANY, ANY],
        out_specs=ANY,
        input_output_aliases={0: 0},
        compiler_params=pltpu.CompilerParams(vmem_limit_bytes=2**20),
        cost_estimate=pl.CostEstimate(flops=1, bytes_accessed=1, transcendentals=0),
        name="after",
    )(block, ready)


def sides(place, width):
    half = place[2]
    mine = pl.ds(pl.multiple_of(half * width, width), width)
    other = pl.ds(pl.multiple_of((1 - half) * width, width), width)
    return mine, other


def gates_body(place, slot_expert, slot_tokens, slot_gate, cot, gate_own, gate_next, scaled):
    slots, block = slot_tokens.shape
    count = cot.shape[0]
    token = lax.broadcasted_iota(jnp.int32, (count, block), 0)
    own = jnp.zeros((count, block), F32)
    following = jnp.zeros((count, block), F32)
    for slot in range(slots):
        expert = slot_expert[slot]
        gates = slot_gate[pl.ds(slot, 1), :]
        hit = token == slot_tokens[pl.ds(slot, 1), :]
        own += jnp.where(hit, jnp.where(expert == place[0], gates, 0.0), 0.0)
        following += jnp.where(hit, jnp.where(expert == place[1], gates, 0.0), 0.0)
    gate_own[...] = jnp.sum(own, axis=1, keepdims=True)
    column = jnp.sum(following, axis=1, keepdims=True)
    gate_next[...] = column
    scaled[...] = (column * cot[...].astype(F32)).astype(BF16)


def forward(tok_mine, tok_other, w_first, w_second, mine, other):
    gate_pre = matmul(tok_mine, w_first[mine, :]) + matmul(tok_other, w_first[other, :])
    up_pre = matmul(tok_mine, w_second[mine, :]) + matmul(tok_other, w_second[other, :])
    sigmoid_value = 1.0 / (1.0 + jnp.exp(-gate_pre))
    active = gate_pre * sigmoid_value
    slope_term = sigmoid_value * (1.0 + gate_pre * (1.0 - sigmoid_value))
    return active, up_pre * slope_term, (active * up_pre).astype(BF16)


def backward(cot_mine, cot_other, w_third, mine, other, active, slope_up):
    back_hidden = contract_rows(cot_mine, w_third[:, mine]) + contract_rows(
        cot_other, w_third[:, other]
    )
    return (back_hidden * slope_up).astype(BF16), (back_hidden * active).astype(BF16)


def back_rows(grad_one, grad_two, w_first, w_second, side):
    return contract_rows(grad_one, w_first[side, :]) + contract_rows(grad_two, w_second[side, :])


def own_body(
    place, tok_m, tok_o, cot_m, cot_o, gate, w_first, w_second, w_third,
    out_send, out_keep, back_send, back_keep, grad_first, grad_second, grad_third,
):
    mine, other = sides(place, tok_m.shape[1])
    active, slope_up, hidden = forward(tok_m[...], tok_o[...], w_first, w_second, mine, other)
    column = gate[...]
    out_send[...] = (column * matmul(hidden, w_third[:, other])).astype(BF16)
    out_keep[...] = column * matmul(hidden, w_third[:, mine])
    scaled_m = (column * cot_m[...].astype(F32)).astype(BF16)
    scaled_o = (column * cot_o[...].astype(F32)).astype(BF16)
    one, two = backward(scaled_m, scaled_o, w_third, mine, other, active, slope_up)
    back_send[...] = back_rows(one, two, w_first, w_second, other).astype(BF16)
    back_keep[...] = back_rows(one, two, w_first, w_second, mine)
    grad_first[mine, :] = contract_cols(tok_m[...], one).astype(BF16)
    grad_first[other, :] = contract_cols(tok_o[...], one).astype(BF16)
    grad_second[mine, :] = contract_cols(tok_m[...], two).astype(BF16)
    grad_second[other, :] = contract_cols(tok_o[...], two).astype(BF16)
    grad_third[:, mine] = contract_cols(hidden, scaled_m).astype(BF16)
    grad_third[:, other] = contract_cols(hidden, scaled_o).astype(BF16)


def guest_forward_body(
    place, tok_m, tok_o, w_first, w_second, w_third,
    out_send, out_keep, active_ref, slope_ref, hidden_ref,
):
    mine, other = sides(place, tok_m.shape[1])
    active, slope_up, hidden = forward(tok_m[...], tok_o[...], w_first, w_second, mine, other)
    out_send[...] = matmul(hidden, w_third[:, other]).astype(BF16)
    out_keep[...] = matmul(hidden, w_third[:, mine])
    active_ref[...] = active
    slope_ref[...] = slope_up
    hidden_ref[...] = hidden


def guest_backward_body(
    place, cot_m, cot_o, w_first, w_second, w_third, active, slope_up,
    back_send, back_keep, one_ref, two_ref,
):
    mine, other = sides(place, cot_m.shape[1])
    one, two = backward(cot_m[...], cot_o[...], w_third, mine, other, active[...], slope_up[...])
    back_send[...] = back_rows(one, two, w_first, w_second, other).astype(BF16)
    back_keep[...] = back_rows(one, two, w_first, w_second, mine)
    one_ref[...] = one
    two_ref[...] = two


def grads_body(
    place, tok_m, tok_o, cot_m, cot_o, hidden, one, two, own_first, own_second, own_third, *rest
):
    grad_first, grad_second, grad_third = rest[-3:]
    mine, other = sides(place, tok_m.shape[1])

    def joined(own, lent):
        return (own.astype(F32) + lent.astype(BF16).astype(F32)).astype(BF16)

    for side, tok, cot in ((mine, tok_m, cot_m), (other, tok_o, cot_o)):
        grad_first[0, side, :] = joined(own_first[side, :], contract_cols(tok[...], one[...]))
        grad_second[0, side, :] = joined(own_second[side, :], contract_cols(tok[...], two[...]))
        grad_third[0, :, side] = joined(own_third[:, side], contract_cols(hidden[...], cot[...]))


def on_device(tokens, cotangent, block_tokens, block_expert, block_gate, w_gate, w_up, w_down):
    size = lax.axis_size("blk")
    me = lax.axis_index("blk")
    place = jnp.stack([me, lax.rem(me + 1, size), lax.axis_index("dp")]).astype(jnp.int32)
    weights = (w_gate[0], w_up[0], w_down[0])
    rows = (tokens.shape, F32)
    rows16 = (tokens.shape, BF16)
    units = (tokens.shape[0], w_down.shape[1])
    column = ((tokens.shape[0], 1), F32)

    guest_tokens = passed_along(tokens, "blk", 1)
    gate_own, gate_next, scaled_next = call(
        gates_body, [column, column, rows16], [SMEM, SMEM, VMEM, VMEM, VMEM],
        place, block_expert, block_tokens, block_gate.astype(F32), cotangent,
        name="gates",
    )
    guest_cot = passed_along(scaled_next, "blk", 1)

    out_send, out_keep, back_send, back_keep, *own_grads = call(
        own_body,
        [rows16, rows, rows16, rows] + [(weight.shape, BF16) for weight in weights],
        [SMEM] + [VMEM] * 8,
        place, tokens, partner(tokens), cotangent, partner(cotangent), gate_own, *weights,
        name="own",
    )
    own_out = out_keep + partner(out_send).astype(F32)
    own_back = back_keep + partner(back_send).astype(F32)

    guest_tokens = after(guest_tokens, out_send)
    guest_other = partner(guest_tokens, 4)
    lent_send, lent_keep, active, slope_up, hidden = call(
        guest_forward_body,
        [rows16, rows, (units, F32), (units, F32), (units, BF16)],
        [SMEM] + [VMEM] * 5,
        place, guest_tokens, guest_other, *weights,
        name="guest_forward",
    )
    lent_out = (lent_keep + partner(lent_send, 4).astype(F32)).astype(BF16)
    came_out = passed_along(lent_out, "blk", -1)

    guest_cot = after(guest_cot, lent_out)
    cot_other = partner(guest_cot, 4)
    lent_send, lent_keep, one, two = call(
        guest_backward_body,
        [rows16, rows, (units, BF16), (units, BF16)],
        [SMEM] + [VMEM] * 7,
        place, guest_cot, cot_other, *weights, active, slope_up,
        name="guest_backward",
    )
    lent_back = (lent_keep + partner(lent_send, 2).astype(F32)).astype(BF16)
    came_back = passed_along(lent_back, "blk", -1)
    outputs = (own_out + gate_next * came_out.astype(F32)).astype(BF16)
    grads = call(
        grads_body,
        [(weight.shape, BF16) for weight in (w_gate, w_up, w_down)],
        [SMEM] + [VMEM] * 10 + [ANY, ANY],
        place, guest_tokens, guest_other, guest_cot, cot_other, hidden, one, two, *own_grads,
        lent_back, outputs,
        name="grads", flops=30*10**9,
    )
    backs = own_back + came_back.astype(F32)
    return (outputs, backs.astype(BF16), *grads)


def solution(mesh):
    in_specs = (
        P("blk", "dp"),
        P("blk", "dp"),
        P("blk", None),
        P("blk"),
        P("blk", None),
        P("blk", None, "dp"),
        P("blk", None, "dp"),
        P("blk", "dp", None),
    )
    out_specs = (
        P("blk", "dp"),
        P("blk", "dp"),
        P("blk", None, "dp"),
        P("blk", None, "dp"),
        P("blk", "dp", None),
    )
    return jax.shard_map(
        on_device, mesh=mesh, in_specs=in_specs, out_specs=out_specs, check_vma=False
    )
```

```python
import jax
import jax.numpy as jnp
from jax import lax
from jax.experimental import pallas as pl
from jax.experimental.pallas import tpu as pltpu
from jax.sharding import PartitionSpec as P

BF16 = jnp.bfloat16
F32 = jnp.float32
VMEM = pl.BlockSpec(memory_space=pltpu.VMEM)
SMEM = pl.BlockSpec(memory_space=pltpu.SMEM)
ANY = pl.BlockSpec(memory_space=pl.ANY)


def passed_along(block, axis, distance):
    size = lax.axis_size(axis)
    return lax.ppermute(block, axis, [((i - distance) % size, i) for i in range(size)])


def partner(block, pieces=1):
    if pieces == 1:
        return passed_along(block, "dp", 1)
    step = block.shape[0] // pieces
    swapped = [
        passed_along(block[i * step : (i + 1) * step], "dp", 1) for i in range(pieces)
    ]
    return jnp.concatenate(swapped, axis=0)


def returned(keep, send, pieces, cuts):
    step = keep.shape[0] // pieces
    parts = []
    for count in cuts:
        first = len(parts) and sum(part.shape[0] for part in parts)
        rows = slice(first, first + count * step)
        other = partner(send[rows], count)
        parts.append((keep[rows] + other.astype(F32)).astype(BF16))
    return parts, jnp.concatenate([passed_along(part, "blk", -1) for part in parts], axis=0)


def matmul(left_side, right_side):
    return jnp.dot(left_side, right_side, preferred_element_type=F32)


def contract_rows(left_side, right_side):
    return lax.dot_general(
        left_side, right_side, (((1,), (1,)), ((), ())), preferred_element_type=F32
    )


def contract_cols(left_side, right_side):
    return lax.dot_general(
        left_side, right_side, (((0,), (0,)), ((), ())), preferred_element_type=F32
    )


def call(body, outs, specs, *operands, name, limit=48, flops=1):
    return pl.pallas_call(
        body,
        out_shape=[jax.ShapeDtypeStruct(shape, kind) for shape, kind in outs],
        in_specs=specs,
        out_specs=[VMEM] * len(outs),
        compiler_params=pltpu.CompilerParams(vmem_limit_bytes=limit * 2**20),
        cost_estimate=pl.CostEstimate(flops=flops, bytes_accessed=1, transcendentals=0),
        name=name,
    )(*operands)


def after(block, *ready):
    return pl.pallas_call(
        lambda *refs: None,
        out_shape=jax.ShapeDtypeStruct(block.shape, block.dtype),
        in_specs=[ANY] * (1 + len(ready)),
        out_specs=ANY,
        input_output_aliases={0: 0},
        compiler_params=pltpu.CompilerParams(vmem_limit_bytes=2**20),
        cost_estimate=pl.CostEstimate(flops=1, bytes_accessed=1, transcendentals=0),
        name="after",
    )(block, *ready)


def sides(place, width):
    half = place[2]
    mine = pl.ds(pl.multiple_of(half * width, width), width)
    other = pl.ds(pl.multiple_of((1 - half) * width, width), width)
    return mine, other


def gates_body(place, slot_expert, slot_tokens, slot_gate, cot, gate_own, gate_next, scaled):
    slots, block = slot_tokens.shape
    count = cot.shape[0]
    token = lax.broadcasted_iota(jnp.int32, (count, block), 0)
    own = jnp.zeros((count, block), F32)
    following = jnp.zeros((count, block), F32)
    for slot in range(slots):
        expert = slot_expert[slot]
        gates = slot_gate[pl.ds(slot, 1), :]
        hit = token == slot_tokens[pl.ds(slot, 1), :]
        own += jnp.where(hit, jnp.where(expert == place[0], gates, 0.0), 0.0)
        following += jnp.where(hit, jnp.where(expert == place[1], gates, 0.0), 0.0)
    gate_own[...] = jnp.sum(own, axis=1, keepdims=True)
    column = jnp.sum(following, axis=1, keepdims=True)
    gate_next[...] = column
    scaled[pl.ds(0, count), :] = (column * cot[...].astype(F32)).astype(BF16)
    if 0:
        scaled[pl.ds(count, 0), :] = jnp.zeros((0, cot.shape[1]), BF16)


def forward(tok_mine, tok_other, w_first, w_second, mine, other):
    gate_pre = matmul(tok_mine, w_first[mine, :]) + matmul(tok_other, w_first[other, :])
    up_pre = matmul(tok_mine, w_second[mine, :]) + matmul(tok_other, w_second[other, :])
    sigmoid_value = 1.0 / (1.0 + jnp.exp(-gate_pre))
    active = gate_pre * sigmoid_value
    slope_term = sigmoid_value * (1.0 + gate_pre * (1.0 - sigmoid_value))
    return active, up_pre * slope_term, (active * up_pre).astype(BF16)


def backward(cot_mine, cot_other, w_third, mine, other, active, slope_up):
    back_hidden = contract_rows(cot_mine, w_third[:, mine]) + contract_rows(
        cot_other, w_third[:, other]
    )
    return (back_hidden * slope_up).astype(BF16), (back_hidden * active).astype(BF16)


def back_rows(grad_one, grad_two, w_first, w_second, side):
    return contract_rows(grad_one, w_first[side, :]) + contract_rows(grad_two, w_second[side, :])


def own_body(
    place, tok_m, tok_o, cot_m, cot_o, gate, w_first, w_second, w_third,
    out_send, out_keep, back_send, back_keep, grad_first, grad_second, grad_third,
):
    mine, other = sides(place, tok_m.shape[1])
    active, slope_up, hidden = forward(tok_m[...], tok_o[...], w_first, w_second, mine, other)
    column = gate[...]
    out_send[...] = (column * matmul(hidden, w_third[:, other])).astype(BF16)
    out_keep[...] = column * matmul(hidden, w_third[:, mine])
    scaled_m = (column * cot_m[...].astype(F32)).astype(BF16)
    scaled_o = (column * cot_o[...].astype(F32)).astype(BF16)
    one, two = backward(scaled_m, scaled_o, w_third, mine, other, active, slope_up)
    back_send[...] = back_rows(one, two, w_first, w_second, other).astype(BF16)
    back_keep[...] = back_rows(one, two, w_first, w_second, mine)
    grad_first[mine, :] = contract_cols(tok_m[...], one).astype(BF16)
    grad_first[other, :] = contract_cols(tok_o[...], one).astype(BF16)
    grad_second[mine, :] = contract_cols(tok_m[...], two).astype(BF16)
    grad_second[other, :] = contract_cols(tok_o[...], two).astype(BF16)
    grad_third[:, mine] = contract_cols(hidden, scaled_m).astype(BF16)
    grad_third[:, other] = contract_cols(hidden, scaled_o).astype(BF16)


def guest_forward_body(
    place, tok_m, tok_o, w_first, w_second, w_third,
    out_send, out_keep, active_ref, slope_ref, hidden_ref,
):
    mine, other = sides(place, tok_m.shape[1])
    active, slope_up, hidden = forward(tok_m[...], tok_o[...], w_first, w_second, mine, other)
    out_send[...] = matmul(hidden, w_third[:, other]).astype(BF16)
    out_keep[...] = matmul(hidden, w_third[:, mine])
    active_ref[...] = active
    slope_ref[...] = slope_up
    hidden_ref[...] = hidden


def guest_backward_body(
    place, cot_m, cot_o, w_first, w_second, w_third, active, slope_up,
    *rest
):
    back_send, back_keep, one_ref, two_ref = rest[-4:]
    mine, other = sides(place, cot_m.shape[1])
    one, two = backward(cot_m[...], cot_o[...], w_third, mine, other, active[...], slope_up[...])
    back_send[...] = back_rows(one, two, w_first, w_second, other).astype(BF16)
    back_keep[...] = back_rows(one, two, w_first, w_second, mine)
    one_ref[...] = one
    two_ref[...] = two


def grads_body(
    place, tok_m, tok_o, cot_m, cot_o, hidden, one, two, own_first, own_second, own_third, *rest
):
    grad_first, grad_second, grad_third = rest[-3:]
    mine, other = sides(place, tok_m.shape[1])

    def joined(own, lent):
        return (own.astype(F32) + lent.astype(BF16).astype(F32)).astype(BF16)

    for side, tok, cot in ((mine, tok_m, cot_m), (other, tok_o, cot_o)):
        grad_first[0, side, :] = joined(own_first[side, :], contract_cols(tok[...], one[...]))
        grad_second[0, side, :] = joined(own_second[side, :], contract_cols(tok[...], two[...]))
        grad_third[0, :, side] = joined(own_third[:, side], contract_cols(hidden[...], cot[...]))


def on_device(tokens, cotangent, block_tokens, block_expert, block_gate, w_gate, w_up, w_down):
    size = lax.axis_size("blk")
    me = lax.axis_index("blk")
    place = jnp.stack([me, lax.rem(me + 1, size), lax.axis_index("dp")]).astype(jnp.int32)
    weights = (w_gate[0], w_up[0], w_down[0])
    rows = (tokens.shape, F32)
    rows16 = (tokens.shape, BF16)
    units = (tokens.shape[0], w_down.shape[1])
    column = ((tokens.shape[0], 1), F32)

    guest_tokens = passed_along(tokens, "blk", 1)
    gate_own, gate_next, scaled_next = call(
        gates_body, [column, column, ((tokens.shape[0] + 0, tokens.shape[1]), BF16)], [SMEM, SMEM, VMEM, VMEM, VMEM],
        place, block_expert, block_tokens, block_gate.astype(F32), cotangent,
        name="gates",
    )
    guest_cot = passed_along(scaled_next, "blk", 1)

    out_send, out_keep, back_send, back_keep, *own_grads = call(
        own_body,
        [rows16, rows, rows16, rows] + [(weight.shape, BF16) for weight in weights],
        [SMEM] + [VMEM] * 8,
        place, tokens, partner(tokens), cotangent, partner(cotangent), gate_own, *weights,
        name="own",
    )
    own_out = out_keep + partner(out_send).astype(F32)
    own_back = back_keep + partner(back_send).astype(F32)

    guest_tokens = after(guest_tokens, out_send)
    guest_other = partner(guest_tokens, 2)
    lent_send, lent_keep, active, slope_up, hidden = call(
        guest_forward_body,
        [rows16, rows, (units, F32), (units, F32), (units, BF16)],
        [SMEM] + [VMEM] * 5,
        place, guest_tokens, guest_other, *weights,
        name="guest_forward",
    )
    lent_out, came_out = returned(lent_keep, lent_send, 1, (1,))

    guest_cot = after(guest_cot, lent_send)[: tokens.shape[0]]
    cot_other = partner(guest_cot, 2)
    lent_send, lent_keep, one, two = call(
        guest_backward_body,
        [rows16, rows, (units, BF16), (units, BF16)],
        [SMEM] + [VMEM] * 7 + [ANY] * len(lent_out),
        place, guest_cot, cot_other, *weights, active, slope_up, *lent_out,
        name="guest_backward", flops=1,
    )
    lent_back, came_back = returned(lent_keep, lent_send, 4, (4,))
    outputs = (own_out + gate_next * came_out.astype(F32)).astype(BF16)
    grads = call(
        grads_body,
        [(weight.shape, BF16) for weight in (w_gate, w_up, w_down)],
        [SMEM] + [VMEM] * 10 + [ANY] * (1 + len(lent_back)),
        place, guest_tokens, guest_other, guest_cot, cot_other, hidden, one, two, *own_grads,
        *lent_back, outputs,
        name="grads", flops=100*10**9,
    )
    backs = own_back + came_back.astype(F32)
    return (outputs, backs.astype(BF16), *grads)


def solution(mesh):
    in_specs = (
        P("blk", "dp"),
        P("blk", "dp"),
        P("blk", None),
        P("blk"),
        P("blk", None),
        P("blk", None, "dp"),
        P("blk", None, "dp"),
        P("blk", "dp", None),
    )
    out_specs = (
        P("blk", "dp"),
        P("blk", "dp"),
        P("blk", None, "dp"),
        P("blk", None, "dp"),
        P("blk", "dp", None),
    )
    return jax.shard_map(
        on_device, mesh=mesh, in_specs=in_specs, out_specs=out_specs, check_vma=False
    )
```

```python
import jax
import jax.numpy as jnp
from jax import lax
from jax.experimental import pallas as pl
from jax.experimental.pallas import tpu as pltpu
from jax.sharding import PartitionSpec as P

BF16 = jnp.bfloat16
F32 = jnp.float32
VMEM = pl.BlockSpec(memory_space=pltpu.VMEM)
SMEM = pl.BlockSpec(memory_space=pltpu.SMEM)
ANY = pl.BlockSpec(memory_space=pl.ANY)


def passed_along(block, axis, distance):
    size = lax.axis_size(axis)
    return lax.ppermute(block, axis, [((i - distance) % size, i) for i in range(size)])


def partner(block, pieces=1):
    if pieces == 1:
        return passed_along(block, "dp", 1)
    step = block.shape[0] // pieces
    swapped = [
        passed_along(block[i * step : (i + 1) * step], "dp", 1) for i in range(pieces)
    ]
    return jnp.concatenate(swapped, axis=0)


def returned(keep, send, pieces, cuts):
    step = keep.shape[0] // pieces
    parts = []
    for count in cuts:
        first = len(parts) and sum(part.shape[0] for part in parts)
        rows = slice(first, first + count * step)
        other = partner(send[rows], count)
        parts.append((keep[rows] + other.astype(F32)).astype(BF16))
    return parts, jnp.concatenate([passed_along(part, "blk", -1) for part in parts], axis=0)


def matmul(left_side, right_side):
    return jnp.dot(left_side, right_side, preferred_element_type=F32)


def contract_rows(left_side, right_side):
    return lax.dot_general(
        left_side, right_side, (((1,), (1,)), ((), ())), preferred_element_type=F32
    )


def contract_cols(left_side, right_side):
    return lax.dot_general(
        left_side, right_side, (((0,), (0,)), ((), ())), preferred_element_type=F32
    )


def call(body, outs, specs, *operands, name, limit=48, flops=1):
    return pl.pallas_call(
        body,
        out_shape=[jax.ShapeDtypeStruct(shape, kind) for shape, kind in outs],
        in_specs=specs,
        out_specs=[VMEM] * len(outs),
        compiler_params=pltpu.CompilerParams(vmem_limit_bytes=limit * 2**20),
        cost_estimate=pl.CostEstimate(flops=flops, bytes_accessed=1, transcendentals=0),
        name=name,
    )(*operands)


def after(block, *ready):
    return pl.pallas_call(
        lambda *refs: None,
        out_shape=jax.ShapeDtypeStruct(block.shape, block.dtype),
        in_specs=[ANY] * (1 + len(ready)),
        out_specs=ANY,
        input_output_aliases={0: 0},
        compiler_params=pltpu.CompilerParams(vmem_limit_bytes=2**20),
        cost_estimate=pl.CostEstimate(flops=1, bytes_accessed=1, transcendentals=0),
        name="after",
    )(block, *ready)


def sides(place, width):
    half = place[2]
    mine = pl.ds(pl.multiple_of(half * width, width), width)
    other = pl.ds(pl.multiple_of((1 - half) * width, width), width)
    return mine, other


def gates_body(place, slot_expert, slot_tokens, slot_gate, cot, gate_own, gate_next, scaled):
    slots, block = slot_tokens.shape
    count = cot.shape[0]
    token = lax.broadcasted_iota(jnp.int32, (count, block), 0)
    own = jnp.zeros((count, block), F32)
    following = jnp.zeros((count, block), F32)
    for slot in range(slots):
        expert = slot_expert[slot]
        gates = slot_gate[pl.ds(slot, 1), :]
        hit = token == slot_tokens[pl.ds(slot, 1), :]
        own += jnp.where(hit, jnp.where(expert == place[0], gates, 0.0), 0.0)
        following += jnp.where(hit, jnp.where(expert == place[1], gates, 0.0), 0.0)
    gate_own[...] = jnp.sum(own, axis=1, keepdims=True)
    column = jnp.sum(following, axis=1, keepdims=True)
    gate_next[...] = column
    scaled[pl.ds(0, count), :] = (column * cot[...].astype(F32)).astype(BF16)
    if 0:
        scaled[pl.ds(count, 0), :] = jnp.zeros((0, cot.shape[1]), BF16)


def forward(tok_mine, tok_other, w_first, w_second, mine, other):
    gate_pre = matmul(tok_mine, w_first[mine, :]) + matmul(tok_other, w_first[other, :])
    up_pre = matmul(tok_mine, w_second[mine, :]) + matmul(tok_other, w_second[other, :])
    sigmoid_value = 1.0 / (1.0 + jnp.exp(-gate_pre))
    active = gate_pre * sigmoid_value
    slope_term = sigmoid_value * (1.0 + gate_pre * (1.0 - sigmoid_value))
    return active, up_pre * slope_term, (active * up_pre).astype(BF16)


def backward(cot_mine, cot_other, w_third, mine, other, active, slope_up):
    back_hidden = contract_rows(cot_mine, w_third[:, mine]) + contract_rows(
        cot_other, w_third[:, other]
    )
    return (back_hidden * slope_up).astype(BF16), (back_hidden * active).astype(BF16)


def back_rows(grad_one, grad_two, w_first, w_second, side):
    return contract_rows(grad_one, w_first[side, :]) + contract_rows(grad_two, w_second[side, :])


def own_body(
    place, tok_m, tok_o, cot_m, cot_o, gate, w_first, w_second, w_third,
    out_send, out_keep, back_send, back_keep, grad_first, grad_second, grad_third,
):
    mine, other = sides(place, tok_m.shape[1])
    active, slope_up, hidden = forward(tok_m[...], tok_o[...], w_first, w_second, mine, other)
    column = gate[...]
    out_send[...] = (column * matmul(hidden, w_third[:, other])).astype(BF16)
    out_keep[...] = column * matmul(hidden, w_third[:, mine])
    scaled_m = (column * cot_m[...].astype(F32)).astype(BF16)
    scaled_o = (column * cot_o[...].astype(F32)).astype(BF16)
    one, two = backward(scaled_m, scaled_o, w_third, mine, other, active, slope_up)
    back_send[...] = back_rows(one, two, w_first, w_second, other).astype(BF16)
    back_keep[...] = back_rows(one, two, w_first, w_second, mine)
    grad_first[mine, :] = contract_cols(tok_m[...], one).astype(BF16)
    grad_first[other, :] = contract_cols(tok_o[...], one).astype(BF16)
    grad_second[mine, :] = contract_cols(tok_m[...], two).astype(BF16)
    grad_second[other, :] = contract_cols(tok_o[...], two).astype(BF16)
    grad_third[:, mine] = contract_cols(hidden, scaled_m).astype(BF16)
    grad_third[:, other] = contract_cols(hidden, scaled_o).astype(BF16)


def guest_forward_body(
    place, tok_m, tok_o, w_first, w_second, w_third,
    out_send, out_keep, active_ref, slope_ref, hidden_ref,
):
    mine, other = sides(place, tok_m.shape[1])
    active, slope_up, hidden = forward(tok_m[...], tok_o[...], w_first, w_second, mine, other)
    out_send[...] = matmul(hidden, w_third[:, other]).astype(BF16)
    out_keep[...] = matmul(hidden, w_third[:, mine])
    active_ref[...] = active
    slope_ref[...] = slope_up
    hidden_ref[...] = hidden


def guest_backward_body(
    place, cot_m, cot_o, w_first, w_second, w_third, active, slope_up,
    *rest
):
    back_send, back_keep, one_ref, two_ref = rest[-4:]
    mine, other = sides(place, cot_m.shape[1])
    one, two = backward(cot_m[...], cot_o[...], w_third, mine, other, active[...], slope_up[...])
    back_send[...] = back_rows(one, two, w_first, w_second, other).astype(BF16)
    back_keep[...] = back_rows(one, two, w_first, w_second, mine)
    one_ref[...] = one
    two_ref[...] = two


def grads_body(
    place, tok_m, tok_o, cot_m, cot_o, hidden, one, two, own_first, own_second, own_third, *rest
):
    grad_first, grad_second, grad_third = rest[-3:]
    mine, other = sides(place, tok_m.shape[1])

    def joined(own, lent):
        return (own.astype(F32) + lent.astype(BF16).astype(F32)).astype(BF16)

    for side, tok, cot in ((mine, tok_m, cot_m), (other, tok_o, cot_o)):
        grad_first[0, side, :] = joined(own_first[side, :], contract_cols(tok[...], one[...]))
        grad_second[0, side, :] = joined(own_second[side, :], contract_cols(tok[...], two[...]))
        grad_third[0, :, side] = joined(own_third[:, side], contract_cols(hidden[...], cot[...]))


def on_device(tokens, cotangent, block_tokens, block_expert, block_gate, w_gate, w_up, w_down):
    size = lax.axis_size("blk")
    me = lax.axis_index("blk")
    place = jnp.stack([me, lax.rem(me + 1, size), lax.axis_index("dp")]).astype(jnp.int32)
    weights = (w_gate[0], w_up[0], w_down[0])
    rows = (tokens.shape, F32)
    rows16 = (tokens.shape, BF16)
    units = (tokens.shape[0], w_down.shape[1])
    column = ((tokens.shape[0], 1), F32)

    guest_tokens = passed_along(tokens, "blk", 1)
    gate_own, gate_next, scaled_next = call(
        gates_body, [column, column, ((tokens.shape[0] + 0, tokens.shape[1]), BF16)], [SMEM, SMEM, VMEM, VMEM, VMEM],
        place, block_expert, block_tokens, block_gate.astype(F32), cotangent,
        name="gates",
    )
    guest_cot = passed_along(scaled_next, "blk", 1)

    out_send, out_keep, back_send, back_keep, *own_grads = call(
        own_body,
        [rows16, rows, rows16, rows] + [(weight.shape, BF16) for weight in weights],
        [SMEM] + [VMEM] * 8,
        place, tokens, partner(tokens, 2), cotangent, partner(cotangent, 2), gate_own, *weights,
        name="own",
    )
    own_out = out_keep + partner(out_send).astype(F32)
    own_back = back_keep + partner(back_send).astype(F32)

    guest_tokens = after(guest_tokens, out_send)
    guest_other = partner(guest_tokens, 2)
    lent_send, lent_keep, active, slope_up, hidden = call(
        guest_forward_body,
        [rows16, rows, (units, F32), (units, F32), (units, BF16)],
        [SMEM] + [VMEM] * 5,
        place, guest_tokens, guest_other, *weights,
        name="guest_forward",
    )
    lent_out, came_out = returned(lent_keep, lent_send, 1, (1,))

    guest_cot = after(guest_cot, lent_send)[: tokens.shape[0]]
    cot_other = partner(guest_cot, 2)
    lent_send, lent_keep, one, two = call(
        guest_backward_body,
        [rows16, rows, (units, BF16), (units, BF16)],
        [SMEM] + [VMEM] * 7 + [ANY] * len(lent_out),
        place, guest_cot, cot_other, *weights, active, slope_up, *lent_out,
        name="guest_backward", flops=1,
    )
    lent_back, came_back = returned(lent_keep, lent_send, 4, (4,))
    outputs = (own_out + gate_next * came_out.astype(F32)).astype(BF16)
    grads = call(
        grads_body,
        [(weight.shape, BF16) for weight in (w_gate, w_up, w_down)],
        [SMEM] + [VMEM] * 10 + [ANY] * (1 + len(lent_back)),
        place, guest_tokens, guest_other, guest_cot, cot_other, hidden, one, two, *own_grads,
        *lent_back, outputs,
        name="grads", flops=100*10**9,
    )
    backs = own_back + came_back.astype(F32)
    return (outputs, backs.astype(BF16), *grads)


def solution(mesh):
    in_specs = (
        P("blk", "dp"),
        P("blk", "dp"),
        P("blk", None),
        P("blk"),
        P("blk", None),
        P("blk", None, "dp"),
        P("blk", None, "dp"),
        P("blk", "dp", None),
    )
    out_specs = (
        P("blk", "dp"),
        P("blk", "dp"),
        P("blk", None, "dp"),
        P("blk", None, "dp"),
        P("blk", "dp", None),
    )
    return jax.shard_map(
        on_device, mesh=mesh, in_specs=in_specs, out_specs=out_specs, check_vma=False
    )
```
